256 devices in a mesh: head: 16 (over y, x), blk: 16 (over z, core).
Axes of the slice: x: 4, y: 4, z: 8, core: 2. Of those that a mesh axis runs over, the one named last changes fastest.
Arguments:
- queries: bfloat16 [16, 2048, 4096], P('blk', 'head'), may hold values from -120 to 120
- keys: bfloat16 [16, 2048, 1024], P('blk', 'head'), may hold values from -5 to 5
- values: bfloat16 [16, 2048, 1024], P('blk', 'head'), may hold values from -6 to 6
- blocks: int32 [32, 16, 16, 48], P('head', 'blk'), may hold values from -1 to 15, as said below
Outputs:
- attended: bfloat16 [16, 2048, 4096], P('blk', 'head')
The draws below stay inside these ranges and needn't reach their ends.
Inputs may be any that keep to these rules, and one draw needn't show every extreme that they name: `blocks`: entry [i, c', b, c * 3 + j] names a key block of span c (0 to 15) or is -1; the 3 slots of one span never name the same block twice unless -1.
All inputs are finite; a program needn't handle non-finite values.
Results may differ from the reference program's by a relative error of at most 0.0038.
Values may be sent and summed in bfloat16 or wider, within the bound.
A program may use at most 64 MiB of HBM per device.

```python
import jax
import jax.numpy as jnp
from jax import lax

QHEADS = 32
KVHEADS = 8
HEAD_DIM = 128
BLOCK = 128
SLOTS = 3
SPANS = 16
SPAN = 2048
SPAN_BLOCKS = 16


def shared_keys(key):
    base = jax.random.normal(key, (SPANS, SPAN, KVHEADS * HEAD_DIM), jnp.float32)
    return jnp.clip(base, -5.0, 5.0)


def draw_keys(key, part):
    base = shared_keys(key)
    return base.astype(jnp.bfloat16)


def draw_queries(key, part):
    key = jax.random.fold_in(key, 7)
    key_one = jax.random.fold_in(key, 0)
    drawn = jax.random.normal(key_one, (SPANS, SPAN, QHEADS * HEAD_DIM), jnp.float32)
    drawn = jnp.clip(drawn, -5.0, 5.0)
    return drawn.astype(jnp.bfloat16)


def draw_blocks(key, part):
    key = jax.random.fold_in(key, 11)
    key_one, key_two, key_four = jax.random.split(key, 3)
    density = jax.random.randint(key_one, (QHEADS, 1, 1, 1, 1), 1, 11)
    rank_keys = jax.random.randint(key_two, (QHEADS, SPANS, SPAN_BLOCKS, SPANS, SPAN_BLOCKS), 0, 1 << 20)
    rank_keys = rank_keys * SPAN_BLOCKS + jnp.arange(SPAN_BLOCKS, dtype=jnp.int32)
    order = jnp.argsort(rank_keys, axis=-1, stable=True).astype(jnp.int32)
    taken = min(SLOTS, SPAN_BLOCKS)
    cols = order[..., :taken]
    if SLOTS > taken:
        filler = -jnp.ones((QHEADS, SPANS, SPAN_BLOCKS, SPANS, SLOTS - taken), jnp.int32)
        cols = jnp.concatenate([cols, filler], axis=4)
    kept = jax.random.randint(key_four, (QHEADS, SPANS, SPAN_BLOCKS, SPANS, SLOTS), 0, 10) < density
    listed = jnp.where(kept, cols, -1)
    return listed.reshape(QHEADS, SPANS, SPAN_BLOCKS, SPANS * SLOTS).astype(jnp.int32)


def block_levels(rng, extent, cuts, low, top_value):
    loudness = 1.0
    for axis_at, shards_of in cuts:
        heights = jax.random.uniform(jax.random.fold_in(jax.random.fold_in(rng, 6), axis_at), (shards_of,), jnp.float32, low / len(cuts), top_value / len(cuts))
        loudness = loudness * jnp.repeat(jnp.exp(heights), extent[axis_at] // shards_of).reshape((-1,) + (1,) * (len(extent) - 1 - axis_at))
    return loudness


def noise(rng, dims, spread, bound, pieces=(), kind=jnp.bfloat16):
    entries = spread * jax.random.normal(rng, dims, jnp.float32)
    if pieces:
        entries = entries * block_levels(rng, dims, pieces, -0.22, 0.18)
    return jnp.clip(entries, -bound, bound).astype(kind)


def setup_inputs(seed: int = 0) -> dict:
    key_list = jax.random.split(jax.random.key(seed), 5)
    return {
        "queries": draw_queries(jax.random.fold_in(key_list[4], 71), 0),
        "keys": draw_keys(jax.random.fold_in(key_list[4], 71), 0),
        "values": noise(key_list[2], (SPANS, SPAN, KVHEADS * HEAD_DIM), 1.0, 6.0, ((0, 16), (1, 16))),
        "blocks": draw_blocks(jax.random.fold_in(key_list[4], 71), 0),
    }


NEG = -1e30


def tile_terms(scores, allowed, value_tiles):
    masked = jnp.where(allowed, scores, NEG)
    row_max = jnp.max(masked, axis=-1)
    some = jnp.any(allowed, axis=-1)
    probs = jnp.where(allowed, jnp.exp(masked - row_max[..., None]), 0.0)
    row_sum = jnp.sum(probs, axis=-1)
    rounded = probs.astype(jnp.bfloat16)
    out = jnp.einsum("...qk,...kd->...qd", rounded.astype(jnp.float32), value_tiles.astype(jnp.float32))
    return jnp.where(some, row_max, NEG), row_sum, out


def absorb(state, tile_max, tile_sum, tile_out):
    top, total, mixed = state
    new_top = jnp.maximum(top, jnp.max(tile_max, axis=-2))
    keep = jnp.exp(top - new_top)
    scale_t = jnp.exp(tile_max - new_top[..., None, :])
    total = total * keep + jnp.sum(tile_sum * scale_t, axis=-2)
    mixed = mixed * keep[..., None] + jnp.sum(tile_out * scale_t[..., None], axis=-3)
    return new_top, total, mixed


def one_head(q_head, k_head, v_head, list_head):
    scale = HEAD_DIM ** -0.5
    rows = jnp.arange(SPANS * SPAN_BLOCKS, dtype=jnp.int32).reshape(SPANS, SPAN_BLOCKS)
    qf = q_head.astype(jnp.float32)
    scores = jnp.einsum("crqd,crkd->crqk", qf, k_head.astype(jnp.float32)) * scale
    causal = jnp.tril(jnp.ones((BLOCK, BLOCK), dtype=bool))
    state = tile_terms(scores, causal, v_head)
    for span_id in range(SPANS):
        for slot in range(SLOTS):
            cols = list_head[:, :, span_id * SLOTS + slot]
            allowed = (cols >= 0) & (span_id * SPAN_BLOCKS + cols < rows)
            index = jnp.clip(cols, 0, SPAN_BLOCKS - 1).astype(jnp.int32)
            key_tiles = k_head[span_id][index]
            val_tiles = v_head[span_id][index]
            scores = jnp.einsum("crqd,crkd->crqk", qf, key_tiles.astype(jnp.float32)) * scale
            t_max, t_sum, t_out = tile_terms(scores, allowed[..., None, None], val_tiles)
            state = absorb(state, t_max[..., None, :], t_sum[..., None, :], t_out[..., None, :, :])
    top, total, mixed = state
    return (mixed / total[..., None]).astype(jnp.bfloat16)


def reference(queries, keys, values, blocks):
    group = QHEADS // KVHEADS
    q_all = queries.reshape(SPANS, SPAN_BLOCKS, BLOCK, QHEADS, HEAD_DIM).transpose(3, 0, 1, 2, 4)
    k_all = keys.reshape(SPANS, SPAN_BLOCKS, BLOCK, KVHEADS, HEAD_DIM).transpose(3, 0, 1, 2, 4)
    v_all = values.reshape(SPANS, SPAN_BLOCKS, BLOCK, KVHEADS, HEAD_DIM).transpose(3, 0, 1, 2, 4)

    def per_head(items):
        q_head, list_head, head_id = items
        kv_id = (head_id // group).astype(jnp.int32)
        k_head = lax.dynamic_index_in_dim(k_all, kv_id, 0, keepdims=False)
        v_head = lax.dynamic_index_in_dim(v_all, kv_id, 0, keepdims=False)
        return one_head(q_head, k_head, v_head, list_head)

    outs = lax.map(per_head, (q_all, blocks, jnp.arange(QHEADS, dtype=jnp.int32)))
    return outs.transpose(1, 2, 3, 0, 4).reshape(SPANS, SPAN, QHEADS * HEAD_DIM)
```

```python
import functools
import math

import jax
import jax.numpy as jnp
from jax import lax
from jax.experimental import pallas as pl
from jax.experimental.pallas import tpu as pltpu
from jax.sharding import PartitionSpec as P

HD = 128
BLOCK = 128
SLOTS = 3
NB = 16
SPANS = 16
RING = 8
UNROLL = 8
F32 = jnp.float32
BF16 = jnp.bfloat16
LOW = -1e30
OFF = 2e30
SCALE = HD ** (-0.5) * math.log2(math.e)
MESH = pl.DeviceIdType.MESH

ZB = 16
XB = NB - ZB


def dot(a, b):
    return jnp.dot(a, b, preferred_element_type=F32)


def kernel(q_hbm, k_hbm, v_ref, b_hbm, out_ref, *scratch):
    kv = [[scratch[s * 2 + t] for t in range(2)] for s in range(RING)]
    (vt, qbuf, qt, obuf, acc, m_ref, l_ref, lst_v, lst, sem_own, sem_send, sem_o,
     rz, sz, rs, ss, sem_l) = scratch[2 * RING:]
    h = lax.axis_index("head")
    c = lax.axis_index("blk")
    z, core = c // 2, c % 2
    mirror = SPANS - 1 - c
    sib = (h, 2 * z + 1 - core)
    up = (h, lax.rem(c + 2, SPANS))
    down = (h, lax.rem(c + SPANS - 2, SPANS))

    def wait(ref, sem):
        pltpu.make_async_copy(ref, ref, sem).wait()

    def send(src, dst, s_sem, r_sem, dev):
        pltpu.make_async_remote_copy(
            src_ref=src, dst_ref=dst, send_sem=s_sem, recv_sem=r_sem,
            device_id=dev, device_id_type=MESH).start()

    barrier = pltpu.get_barrier_semaphore()

    def hello(dev):
        pl.semaphore_signal(barrier, inc=1, device_id=dev, device_id_type=MESH)

    def greet(j, _):
        hello((lax.rem(h + j, NB), c))
        return 0

    lax.fori_loop(1, NB, greet, 0)

    def greet_mirror(j, _):
        hello((lax.rem(h + j, NB), mirror))
        return 0

    lax.fori_loop(0, NB, greet_mirror, 0)
    hello(sib)
    hello(up)
    hello(down)

    for g in range(8):
        vt[g] = v_ref[:, g * HD:(g + 1) * HD].T
    pl.semaphore_wait(barrier, 34)

    mine = kv[0][0]

    def send_k(j, _):
        p = lax.rem(h + j, NB)
        col = pl.multiple_of((p // 2) * HD, HD)
        send(k_hbm.at[:, pl.ds(col, HD)], mine.at[h], sem_send.at[0], sem_own.at[0], (p, c))
        return 0

    lax.fori_loop(1, NB, send_k, 0)
    own_col = pl.multiple_of((h // 2) * HD, HD)
    pltpu.make_async_copy(k_hbm.at[:, pl.ds(own_col, HD)], mine.at[h], sem_own.at[0]).start()

    def send_v(j, _):
        p = lax.rem(h + j, NB)
        send(vt.at[p // 2], mine.at[NB + h], sem_send.at[1], sem_own.at[1], (p, c))
        return 0

    lax.fori_loop(1, NB, send_v, 0)
    pltpu.make_async_copy(vt.at[h // 2], mine.at[NB + h], sem_own.at[1]).start()

    def q_cols(p, i):
        return pl.ds(pl.multiple_of((2 * p + i) * HD, HD), HD)

    near = lax.rem(h, 2)
    far = 1 - near

    def send_q_near(j, _):
        p = lax.rem(h + j, NB)
        send(q_hbm.at[:, q_cols(p, near)], qbuf.at[0, h], sem_send.at[2], sem_own.at[2], (p, c))
        return 0

    lax.fori_loop(1, NB, send_q_near, 0)
    pltpu.make_async_copy(q_hbm.at[:, q_cols(h, near)], qbuf.at[0, h], sem_own.at[2]).start()

    def send_q_far(j, _):
        p = lax.rem(h + j, NB)
        send(q_hbm.at[:, q_cols(p, far)], qbuf.at[1, h], sem_send.at[3], sem_own.at[3], (p, mirror))
        return 0

    lax.fori_loop(0, NB, send_q_far, 0)

    send(b_hbm, lst_v, sem_l.at[0], sem_l.at[1], (h, mirror))
    pltpu.make_async_copy(b_hbm, lst.at[0], sem_l.at[2]).start()

    def part(s, t, which, first=0, count=NB):
        return kv[s][t].at[pl.ds(which * NB + first, count)]

    def go_up(s, which):
        send(part(s, 0, which), part(s + 1, 0, which), sz.at[0, s, which],
             rz.at[s + 1, which], up)

    def go_down(s, which):
        d = s if s else RING
        send(part(s, 0, which), part(d - 1, 0, which), sz.at[1, s, which],
             rz.at[d - 1, which], down)

    def go_side(s, which):
        send(part(s, 0, which), part(s, 1, which), ss.at[s, which], rs.at[s, which], sib)

    def got(s, which):
        wait(part(s, 0, which), rz.at[s, which])

    def got_side(s):
        for which in range(2):
            wait(part(s, 1, which), rs.at[s, which])

    def span_of(s, t):
        zz = lax.rem(z + RING - s, RING)
        return 2 * zz + (core if t == 0 else 1 - core)

    def row(r):
        group = r // NB
        return group, lax.rem(r, NB)

    def absorb(r, parts, value_tiles):
        m_old = m_ref[r]
        top = m_old
        for s, off in parts:
            top = jnp.maximum(top, jnp.max(s, axis=0, keepdims=True) * SCALE - off)
        keep = jnp.exp2(m_old - top)
        probs = [jnp.exp2(s * SCALE - (top + off)) for s, off in parts]
        total = jnp.sum(functools.reduce(jnp.add, probs), axis=0, keepdims=True)
        out = None
        for p, tile in zip(probs, value_tiles):
            o = dot(tile, p.astype(BF16))
            out = o if out is None else out + o
        acc[r] = acc[r] * keep + out
        l_ref[r] = l_ref[r] * keep + total
        m_ref[r] = top

    def compute(s, t):
        ref = kv[s][t]
        span = span_of(s, t)
        lo = jnp.where(span <= c, 0, NB // UNROLL)
        hi = jnp.where(span <= mirror, 2 * NB // UNROLL, NB // UNROLL)

        def some(it, _):
            for u in range(UNROLL):
                r = it * UNROLL + u
                group, b = row(r)
                i = lax.rem(u + group, 2)
                limit = jnp.where(span < jnp.where(group == 0, c, mirror), NB, b)
                parts, tiles = [], []
                for j in range(SLOTS):
                    e = lst[group, i, b, span * SLOTS + j]
                    off = jnp.where((e >= 0) & (e < limit), 0.0, OFF)
                    at = jnp.clip(e, 0, NB - 1)
                    parts.append((dot(ref[at], qt[r]), off))
                    tiles.append(ref[NB + at])
                absorb(r, parts, tiles)
            return 0

        lax.fori_loop(lo, hi, some, 0)

    def diagonal(s, t, group):
        ref = kv[s][t]

        def some(it, _):
            keys = lax.broadcasted_iota(jnp.int32, (BLOCK, BLOCK), 0)
            toks = lax.broadcasted_iota(jnp.int32, (BLOCK, BLOCK), 1)
            for u in range(4):
                b = it * 4 + u
                r = group * NB + b
                scores = jnp.where(keys <= toks, dot(ref[b], qt[r]), LOW)
                absorb(r, [(scores, 0.0)], [ref[NB + b]])
            return 0

        lax.fori_loop(0, NB // 4, some, 0)

    wait(part(0, 0, 0), sem_own.at[0])
    go_up(0, 0)
    go_down(0, 0)
    go_side(0, 0)
    wait(part(0, 0, 1), sem_own.at[1])
    go_up(0, 1)
    go_down(0, 1)
    go_side(0, 1)

    def init(r, _):
        acc[r] = jnp.zeros((HD, BLOCK), F32)
        m_ref[r] = jnp.full((1, BLOCK), LOW, F32)
        l_ref[r] = jnp.zeros((1, BLOCK), F32)
        return 0

    lax.fori_loop(0, 2 * NB, init, 0)

    def turn(group):
        def one(b, _):
            qt[group * NB + b] = qbuf[group, b].T
            return 0

        lax.fori_loop(0, NB, one, 0)

    wait(qbuf.at[0], sem_own.at[2])
    turn(0)
    diagonal(0, 0, 0)
    wait(qbuf.at[1], sem_own.at[3])
    turn(1)
    wait(lst_v, sem_l.at[1])
    pltpu.make_async_copy(lst_v, lst.at[1], sem_l.at[3]).start()
    pltpu.make_async_copy(b_hbm, lst.at[0], sem_l.at[2]).wait()
    pltpu.make_async_copy(lst_v, lst.at[1], sem_l.at[3]).wait()

    mirror_at = lax.rem(2 * z + 1, RING)

    def step(s, t):
        if t == 1:
            got_side(s)
        compute(s, t)
        if t == 1 and s % 2 == 1:
            @pl.when(mirror_at == s)
            def _():
                diagonal(s, t, 1)

    def poll(s_up, s_down, which):
        got(s_up, which)
        if s_up < 3 or (s_up == 3 and which == 0):
            go_up(s_up, which)
        got(s_down, which)
        if s_down > 5 or (s_down == 5 and which == 1):
            go_down(s_down, which)
        go_side(s_up, which)
        go_side(s_down, which)

    step(0, 0)
    poll(1, 7, 0)
    step(0, 1)
    poll(1, 7, 1)
    step(1, 0)
    step(7, 0)
    poll(2, 6, 0)
    step(1, 1)
    step(7, 1)
    poll(2, 6, 1)
    step(2, 0)
    step(6, 0)
    poll(3, 5, 0)
    step(2, 1)
    step(6, 1)
    poll(3, 5, 1)
    step(3, 0)
    step(5, 0)
    step(3, 1)
    step(5, 1)
    for which in range(2):
        got(4, which)
        go_side(4, which)
    step(4, 0)
    step(4, 1)

    def out_cols(i):
        return pl.ds(pl.multiple_of((2 * h + i) * HD, HD), HD)

    def finish(b, group):
        r = group * NB + b
        obuf[r] = (acc[r] / l_ref[r]).T.astype(BF16)
        i = lax.rem(b + group, 2)
        return obuf.at[r], out_ref.at[:, out_cols(i)]

    def finish_far(j, _):
        b = lax.rem(h + j, NB)
        src, dst = finish(b, 1)
        send(src, dst, sem_o.at[0], sem_o.at[1], (b, mirror))
        return 0

    lax.fori_loop(0, NB, finish_far, 0)

    def finish_near(j, _):
        b = lax.rem(h + j, NB)
        src, dst = finish(b, 0)
        send(src, dst, sem_o.at[0], sem_o.at[1], (b, c))
        return 0

    lax.fori_loop(1, NB, finish_near, 0)
    src, dst = finish(h, 0)
    pltpu.make_async_copy(src, dst, sem_o.at[1]).start()
    wait(out_ref, sem_o.at[1])

    wait(mine.at[pl.ds(0, NB - 1)], sem_send.at[0])
    wait(mine.at[pl.ds(0, NB - 1)], sem_send.at[1])
    wait(qbuf.at[0, pl.ds(0, NB - 1)], sem_send.at[2])
    wait(qbuf.at[1], sem_send.at[3])
    wait(lst_v, sem_l.at[0])
    wait(obuf.at[pl.ds(0, 2 * NB - 1)], sem_o.at[0])
    for s in range(RING):
        for which in range(2):
            wait(part(s, 0, which), ss.at[s, which])
            if s < 3 or (s == 3 and which == 0):
                wait(part(s, 0, which), sz.at[0, s, which])
            if s == 0 or s > 5 or (s == 5 and which == 1):
                wait(part(s, 0, which), sz.at[1, s, which])


def body(queries, keys, values, blocks):
    anywhere = pl.BlockSpec(memory_space=pl.ANY)
    vmem = pl.BlockSpec(memory_space=pltpu.VMEM)
    dma = pltpu.SemaphoreType.DMA
    out = pl.pallas_call(
        kernel,
        out_shape=jax.ShapeDtypeStruct((BLOCK, queries.shape[2]), BF16),
        in_specs=[anywhere, anywhere, vmem, anywhere],
        out_specs=vmem,
        scratch_shapes=[pltpu.VMEM((2 * NB, BLOCK, HD), BF16) for _ in range(2 * RING)] + [
            pltpu.VMEM((8, HD, BLOCK), BF16),
            pltpu.VMEM((2, NB, BLOCK, HD), BF16),
            pltpu.VMEM((2 * NB, HD, BLOCK), BF16),
            pltpu.VMEM((2 * NB, BLOCK, HD), BF16),
            pltpu.VMEM((2 * NB, HD, BLOCK), F32),
            pltpu.VMEM((2 * NB, 1, BLOCK), F32),
            pltpu.VMEM((2 * NB, 1, BLOCK), F32),
            pltpu.VMEM((2, NB, SPANS * SLOTS), jnp.int32),
            pltpu.SMEM((2, 2, NB, SPANS * SLOTS), jnp.int32),
            dma((4,)),
            dma((4,)),
            dma((2,)),
            dma((RING, 2)),
            dma((2, RING, 2)),
            dma((RING, 2)),
            dma((RING, 2)),
            dma((4,)),
        ],
        compiler_params=pltpu.CompilerParams(
            collective_id=0, has_side_effects=True, vmem_limit_bytes=48 * 2**20),
        name="attend",
    )(queries[0], keys[0], values[0], blocks[:, 0])
    return out[None]


def solution(mesh):
    placed = (
        P("blk", "head", None),
        P("blk", "head", None),
        P("blk", "head", None),
        P("head", "blk", None, None),
    )
    return jax.shard_map(
        body, mesh=mesh, in_specs=placed, out_specs=P("blk", "head", None), check_vma=False
    )
```

```python
import functools
import math

import jax
import jax.numpy as jnp
from jax import lax
from jax.experimental import pallas as pl
from jax.experimental.pallas import tpu as pltpu
from jax.sharding import PartitionSpec as P

HD = 128
BLOCK = 128
SLOTS = 3
NB = 16
SPANS = 16
PAIRS = 8
SIDE = 4
F32 = jnp.float32
BF16 = jnp.bfloat16
LOW = -1e30
OFF = 2e30
SCALE = HD ** (-0.5) * math.log2(math.e)
MESH = pl.DeviceIdType.MESH


def dot(a, b):
    return jnp.dot(a, b, preferred_element_type=F32)


def kernel(q_hbm, k_hbm, v_ref, b_ref, out_ref, *scratch):
    kv = [[scratch[j * 2 + t] for t in range(2)] for j in range(PAIRS)]
    (vt, own, qbuf, qt, obuf, acc, m_ref, l_ref, lists, lst_v, lst,
     sem_own, sem_kvs, sem_q, sem_qs, sem_o, sem_l, sem_cp,
     r1, r2, r3, r4, rs, s1, s2, s3, s4, ss) = scratch[2 * PAIRS:]
    h = lax.axis_index("head")
    c = lax.axis_index("blk")
    z, core = c // 2, c % 2
    x, y = h % SIDE, h // SIDE
    sib = (h, 2 * z + 1 - core)
    a = jnp.where(core == 0, x, y)
    b = jnp.where(core == 0, y, x)
    place = b * SIDE + a
    mirrored = a * SIDE + b

    def device(aa, bb):
        aa, bb = lax.rem(aa, SIDE), lax.rem(bb, SIDE)
        return (jnp.where(core == 0, bb * SIDE + aa, aa * SIDE + bb), c)

    a_next, a_prev = device(a + 1, b), device(a + SIDE - 1, b)
    b_next, b_prev = device(a, b + 1), device(a, b + SIDE - 1)

    def wait(ref, sem):
        pltpu.make_async_copy(ref, ref, sem).wait()

    def send(src, dst, s_sem, r_sem, dev):
        pltpu.make_async_remote_copy(
            src_ref=src, dst_ref=dst, send_sem=s_sem, recv_sem=r_sem,
            device_id=dev, device_id_type=MESH).start()

    barrier = pltpu.get_barrier_semaphore()

    def hello(dev):
        pl.semaphore_signal(barrier, inc=1, device_id=dev, device_id_type=MESH)

    def greet(j, _):
        other = lax.rem(c + j, SPANS)
        hello((h, other))
        hello((c, other))
        return 0

    lax.fori_loop(1, SPANS, greet, 0)
    for dev in (a_next, a_prev, b_next, b_prev):
        hello(dev)

    @pl.when(c != h)
    def _():
        hello((c, c))

    for g in range(PAIRS):
        vt[g] = v_ref[:, g * HD:(g + 1) * HD].T
    lists[...] = jnp.zeros(lists.shape, jnp.int32)
    for n in range(NB):
        lists[n, 0:2, 0:SPANS * SLOTS] = b_ref[:, n, :]
    pl.semaphore_wait(barrier, 34 + jnp.where(c != h, 1, 0))

    def chip(n):
        away = jnp.where(n % 2 == 1, (n + 1) // 2, PAIRS - n // 2)
        return lax.rem(z + away, PAIRS)

    def key_cols(g):
        return pl.ds(pl.multiple_of(g * HD, HD), HD)

    def send_kv(n, _):
        g = chip(n)
        send(k_hbm.at[:, key_cols(g)], own.at[z, 0], sem_kvs.at[0], sem_own.at[z], (h, 2 * g + core))
        send(vt.at[g], own.at[z, 1], sem_kvs.at[1], sem_own.at[z], (h, 2 * g + core))
        return 0

    lax.fori_loop(1, PAIRS, send_kv, 0)
    pltpu.make_async_copy(k_hbm.at[:, key_cols(z)], own.at[z, 0], sem_own.at[z]).start()
    pltpu.make_async_copy(vt.at[z], own.at[z, 1], sem_own.at[z]).start()

    def send_list(j, _):
        p = lax.rem(h + j, NB)
        send(lists.at[p], lst_v.at[c], sem_l.at[0], sem_l.at[1], (p, h))
        return 0

    lax.fori_loop(1, NB, send_list, 0)

    @pl.when(c != h)
    def _():
        send(lists.at[h], lst_v.at[c], sem_l.at[2], sem_l.at[1], (h, h))

    @pl.when(c == h)
    def _():
        pltpu.make_async_copy(lists.at[h], lst_v.at[c], sem_l.at[1]).start()

    def q_cols(p):
        return pl.ds(pl.multiple_of(p * 2 * HD, 2 * HD), 2 * HD)

    def send_q(p):
        send(q_hbm.at[:, q_cols(p)], qbuf.at[c], sem_qs.at[0], sem_q.at[c], (h, p))

    pltpu.make_async_copy(q_hbm.at[:, q_cols(c)], qbuf.at[c], sem_q.at[c]).start()
    send_q(2 * z + 1 - core)

    def send_qs(n, _):
        g = chip(n)
        send_q(2 * g)
        send_q(2 * g + 1)
        return 0

    lax.fori_loop(1, PAIRS, send_qs, 0)

    def line(j, t, bb):
        return kv[j][t].at[pl.ds(lax.rem(bb, SIDE) * SIDE, SIDE)]

    def half(j, bb, which):
        return kv[j][0].at[pl.ds(lax.rem(bb, SIDE) * SIDE, SIDE), which]

    def tile(j, aa):
        return kv[j][0].at[b * SIDE + lax.rem(aa, SIDE)]

    def tile_half(j, aa, which):
        return kv[j][0].at[b * SIDE + lax.rem(aa, SIDE), which]

    def aside(j, bb):
        send(line(j, 0, bb), line(j, 1, bb), ss.at[j], rs.at[j], sib)

    def event1(j):
        wait(own.at[j], sem_own.at[j])
        send(own.at[j], kv[j][0].at[place], s1.at[j, 0], r1.at[j, 0], a_next)
        send(own.at[j], kv[j][0].at[place], s1.at[j, 1], r1.at[j, 1], a_prev)
        pltpu.make_async_copy(own.at[j], kv[j][0].at[place], sem_cp.at[j]).start()

    def event2(j):
        wait(tile(j, a + 3), r1.at[j, 0])
        send(tile_half(j, a + 3, 0), tile_half(j, a + 3, 0), s2.at[j, 0], r2.at[j, 0], a_next)
        wait(tile(j, a + 1), r1.at[j, 1])
        send(tile_half(j, a + 1, 1), tile_half(j, a + 1, 1), s2.at[j, 1], r2.at[j, 1], a_prev)

    def event3(j):
        wait(tile_half(j, a + 2, 0), r2.at[j, 0])
        wait(tile_half(j, a + 2, 1), r2.at[j, 1])
        wait(kv[j][0].at[place], sem_cp.at[j])
        send(line(j, 0, b), line(j, 0, b), s3.at[j, 0], r3.at[j, 0], b_next)
        send(line(j, 0, b), line(j, 0, b), s3.at[j, 1], r3.at[j, 1], b_prev)
        aside(j, b)

    def event4(j):
        wait(line(j, 0, b + 3), r3.at[j, 0])
        send(half(j, b + 3, 0), half(j, b + 3, 0), s4.at[j, 0], r4.at[j, 0], b_next)
        wait(line(j, 0, b + 1), r3.at[j, 1])
        send(half(j, b + 1, 1), half(j, b + 1, 1), s4.at[j, 1], r4.at[j, 1], b_prev)
        aside(j, b + 3)
        aside(j, b + 1)

    def event5(j):
        wait(half(j, b + 2, 0), r4.at[j, 0])
        wait(half(j, b + 2, 1), r4.at[j, 1])
        aside(j, b + 2)

    def events(n):
        for late, event in enumerate((event1, event2, event3, event4, event5)):
            if 0 <= n - late < PAIRS:
                event(n - late)

    parity = (core, 1 - core)

    def tiles_of(j, cc, i):
        parts = []
        for t in range(2):
            span = 2 * j + parity[t]
            limit = jnp.where(span < cc, NB, jnp.where(span == cc, h, 0))
            for n in range(SLOTS):
                e = lst[cc, i, span * SLOTS + n]
                off = jnp.where((e >= 0) & (e < limit), 0.0, OFF)
                e = jnp.clip(e, 0, NB - 1)
                at = jnp.where(parity[t] == 0, e, (e % SIDE) * SIDE + e // SIDE)
                scores = dot(kv[j][t][at, 0], qt[cc, i])
                parts.append((scores, off, kv[j][t][at, 1]))
        return parts

    def absorb(cc, i, parts, first):
        top = jnp.full((1, BLOCK), LOW, F32) if first else m_ref[cc, i]
        m_old = top
        for s, off, _ in parts:
            top = jnp.maximum(top, jnp.max(s, axis=0, keepdims=True) * SCALE - off)
        probs = [jnp.exp2(s * SCALE - (top + off)) for s, off, _ in parts]
        total = jnp.sum(functools.reduce(jnp.add, probs), axis=0, keepdims=True)
        out = None
        for p, (_, _, values) in zip(probs, parts):
            o = dot(values, p.astype(BF16))
            out = o if out is None else out + o
        if not first:
            keep = jnp.exp2(m_old - top)
            total = l_ref[cc, i] * keep + total
            out = acc[cc, i] * keep + out
        return top, total, out

    def later_rows(j, pair):
        for u in range(2):
            for i in range(2):
                cc = 2 * pair + u
                top, total, out = absorb(cc, i, tiles_of(j, cc, i), j == 0)
                m_ref[cc, i] = top
                l_ref[cc, i] = total
                acc[cc, i] = out

    def out_cols(p):
        return pl.ds(pl.multiple_of(p * 2 * HD, 2 * HD), 2 * HD)

    def last_rows(j):
        keys = lax.broadcasted_iota(jnp.int32, (BLOCK, BLOCK), 0)
        toks = lax.broadcasted_iota(jnp.int32, (BLOCK, BLOCK), 1)
        for t in range(2):
            cc = 2 * j + parity[t]
            here = place if t == 0 else mirrored
            for i in range(2):
                scores = jnp.where(keys <= toks, dot(kv[j][t][here, 0], qt[cc, i]), LOW)
                parts = tiles_of(j, cc, i) + [(scores, 0.0, kv[j][t][here, 1])]
                _, total, out = absorb(cc, i, parts, j == 0)
                obuf[cc, :, i * HD:(i + 1) * HD] = (out / total).T.astype(BF16)
        for t in range(2):
            cc = 2 * j + parity[t]

            @pl.when(cc != c)
            def _():
                send(obuf.at[cc], out_ref.at[:, out_cols(c)], sem_o.at[0], sem_o.at[1], (h, cc))

            @pl.when(cc == c)
            def _():
                pltpu.make_async_copy(obuf.at[cc], out_ref.at[:, out_cols(c)], sem_o.at[1]).start()

    def turn(cc):
        wait(qbuf.at[cc], sem_q.at[cc])
        for i in range(2):
            qt[cc, i] = qbuf[cc, :, i * HD:(i + 1) * HD].T

    for n in range(5):
        events(n)
    wait(lst_v, sem_l.at[1])
    pltpu.make_async_copy(lst_v, lst, sem_l.at[3]).start()
    pltpu.make_async_copy(lst_v, lst, sem_l.at[3]).wait()

    plan = {0: {1: 5, 4: 6, 6: 7}, 1: {1: 8, 3: 9, 5: 10}, 2: {1: 11}}
    for j in range(PAIRS):
        wait(kv[j][1], rs.at[j])
        marks = plan.get(j, {})
        if j == 0:
            def some(n, _):
                pair = chip(n)
                turn(2 * pair)
                turn(2 * pair + 1)

                @pl.when(pair != 0)
                def _():
                    later_rows(0, pair)

                for at, step in marks.items():
                    @pl.when(n == at)
                    def _():
                        events(step)
                return 0

            lax.fori_loop(0, PAIRS, some, 0)
            last_rows(0)
        else:
            last_rows(j)
            if j + 1 < PAIRS:
                def some(pair, _):
                    later_rows(j, pair)
                    for at, step in marks.items():
                        @pl.when(pair == j + at)
                        def _():
                            events(step)
                    return 0

                lax.fori_loop(j + 1, PAIRS, some, 0)

    wait(out_ref, sem_o.at[1])

    wait(own.at[pl.ds(0, PAIRS - 1), 0], sem_kvs.at[0])
    wait(own.at[pl.ds(0, PAIRS - 1), 1], sem_kvs.at[1])
    wait(lists.at[pl.ds(0, NB - 1)], sem_l.at[0])

    @pl.when(c != h)
    def _():
        wait(lists.at[0], sem_l.at[2])

    wait(qbuf.at[pl.ds(0, SPANS - 1)], sem_qs.at[0])
    wait(obuf.at[pl.ds(0, SPANS - 1)], sem_o.at[0])
    for j in range(PAIRS):
        for n in range(2):
            wait(own.at[j], s1.at[j, n])
            wait(tile_half(j, a, n), s2.at[j, n])
            wait(line(j, 0, b), s3.at[j, n])
            wait(half(j, b, n), s4.at[j, n])
        wait(kv[j][0], ss.at[j])


def body(queries, keys, values, blocks):
    anywhere = pl.BlockSpec(memory_space=pl.ANY)
    vmem = pl.BlockSpec(memory_space=pltpu.VMEM)
    dma = pltpu.SemaphoreType.DMA
    events = [dma((PAIRS, 2)) for _ in range(4)] + [dma((PAIRS,))]
    out = pl.pallas_call(
        kernel,
        out_shape=jax.ShapeDtypeStruct((BLOCK, queries.shape[2]), BF16),
        in_specs=[anywhere, anywhere, vmem, vmem],
        out_specs=vmem,
        scratch_shapes=[pltpu.VMEM((NB, 2, BLOCK, HD), BF16) for _ in range(2 * PAIRS)] + [
            pltpu.VMEM((PAIRS, HD, BLOCK), BF16),
            pltpu.VMEM((PAIRS, 2, BLOCK, HD), BF16),
            pltpu.VMEM((SPANS, BLOCK, 2 * HD), BF16),
            pltpu.VMEM((SPANS, 2, HD, BLOCK), BF16),
            pltpu.VMEM((SPANS, BLOCK, 2 * HD), BF16),
            pltpu.VMEM((SPANS, 2, HD, BLOCK), F32),
            pltpu.VMEM((SPANS, 2, 1, BLOCK), F32),
            pltpu.VMEM((SPANS, 2, 1, BLOCK), F32),
            pltpu.VMEM((NB, 8, 128), jnp.int32),
            pltpu.VMEM((SPANS, 8, 128), jnp.int32),
            pltpu.SMEM((SPANS, 8, 128), jnp.int32),
            dma((PAIRS,)),
            dma((2,)),
            dma((SPANS,)),
            dma((1,)),
            dma((2,)),
            dma((4,)),
            dma((PAIRS,)),
        ] + events + events,
        compiler_params=pltpu.CompilerParams(
            collective_id=0, has_side_effects=True, vmem_limit_bytes=48 * 2**20),
        name="attend",
    )(queries[0], keys[0], values[0], blocks[:, 0])
    return out[None]


def solution(mesh):
    placed = (
        P("blk", "head", None),
        P("blk", "head", None),
        P("blk", "head", None),
        P("head", "blk", None, None),
    )
    return jax.shard_map(
        body, mesh=mesh, in_specs=placed, out_specs=P("blk", "head", None), check_vma=False
    )
```

```python
import functools
import math

import jax
import jax.numpy as jnp
from jax import lax
from jax.experimental import pallas as pl
from jax.experimental.pallas import tpu as pltpu
from jax.sharding import PartitionSpec as P

HD = 128
BLOCK = 128
SLOTS = 3
NB = 16
SPANS = 16
PAIRS = 8
SIDE = 4
F32 = jnp.float32
BF16 = jnp.bfloat16
LOW = -1e30
OFF = 2e30
SCALE = HD ** (-0.5) * math.log2(math.e)
MESH = pl.DeviceIdType.MESH


def dot(a, b):
    return jnp.dot(a, b, preferred_element_type=F32)


def kernel(q_hbm, k_hbm, v_ref, b_ref, out_ref, *scratch):
    kv = [[scratch[j * 2 + t] for t in range(2)] for j in range(PAIRS)]
    (vt, own, qbuf, qt, obuf, acc, m_ref, l_ref, lists, lst_v, lst,
     sem_own, sem_kvs, sem_q, sem_qs, sem_o, sem_l, sem_cp,
     r1, r2, r3, r4, rs, s1, s2, s3, s4, ss) = scratch[2 * PAIRS:]
    h = lax.axis_index("head")
    c = lax.axis_index("blk")
    z, core = c // 2, c % 2
    x, y = h % SIDE, h // SIDE
    sib = (h, 2 * z + 1 - core)
    a = jnp.where(core == 0, x, y)
    b = jnp.where(core == 0, y, x)
    place = b * SIDE + a
    mirrored = a * SIDE + b

    def device(aa, bb):
        aa, bb = lax.rem(aa, SIDE), lax.rem(bb, SIDE)
        return (jnp.where(core == 0, bb * SIDE + aa, aa * SIDE + bb), c)

    a_next, a_prev = device(a + 1, b), device(a + SIDE - 1, b)
    b_next, b_prev = device(a, b + 1), device(a, b + SIDE - 1)

    def wait(ref, sem):
        pltpu.make_async_copy(ref, ref, sem).wait()

    def send(src, dst, s_sem, r_sem, dev):
        pltpu.make_async_remote_copy(
            src_ref=src, dst_ref=dst, send_sem=s_sem, recv_sem=r_sem,
            device_id=dev, device_id_type=MESH).start()

    barrier = pltpu.get_barrier_semaphore()

    def hello(dev):
        pl.semaphore_signal(barrier, inc=1, device_id=dev, device_id_type=MESH)

    def greet(j, _):
        other = lax.rem(c + j, SPANS)
        hello((h, other))
        hello((c, other))
        return 0

    lax.fori_loop(1, SPANS, greet, 0)
    for dev in (a_next, a_prev, b_next, b_prev):
        hello(dev)

    @pl.when(c != h)
    def _():
        hello((c, c))

    for g in range(PAIRS):
        vt[g] = v_ref[:, g * HD:(g + 1) * HD].T
    lists[...] = jnp.zeros(lists.shape, jnp.int32)
    for n in range(NB):
        lists[n, 0:2, 0:SPANS * SLOTS] = b_ref[:, n, :]
    pl.semaphore_wait(barrier, 34 + jnp.where(c != h, 1, 0))

    def chip(n):
        away = jnp.where(n % 2 == 1, (n + 1) // 2, PAIRS - n // 2)
        return lax.rem(z + away, PAIRS)

    def key_cols(g):
        return pl.ds(pl.multiple_of(g * HD, HD), HD)

    def send_kv(n, _):
        g = chip(n)
        send(k_hbm.at[:, key_cols(g)], own.at[z, 0], sem_kvs.at[0], sem_own.at[z], (h, 2 * g + core))
        send(vt.at[g], own.at[z, 1], sem_kvs.at[1], sem_own.at[z], (h, 2 * g + core))
        return 0

    lax.fori_loop(1, PAIRS, send_kv, 0)
    pltpu.make_async_copy(k_hbm.at[:, key_cols(z)], own.at[z, 0], sem_own.at[z]).start()
    pltpu.make_async_copy(vt.at[z], own.at[z, 1], sem_own.at[z]).start()

    def send_list(j, _):
        p = lax.rem(h + j, NB)
        send(lists.at[p], lst_v.at[c], sem_l.at[0], sem_l.at[1], (p, h))
        return 0

    lax.fori_loop(1, NB, send_list, 0)

    @pl.when(c != h)
    def _():
        send(lists.at[h], lst_v.at[c], sem_l.at[2], sem_l.at[1], (h, h))

    @pl.when(c == h)
    def _():
        pltpu.make_async_copy(lists.at[h], lst_v.at[c], sem_l.at[1]).start()

    def q_cols(p):
        return pl.ds(pl.multiple_of(p * 2 * HD, 2 * HD), 2 * HD)

    def send_q(p):
        send(q_hbm.at[:, q_cols(p)], qbuf.at[c], sem_qs.at[0], sem_q.at[c], (h, p))

    pltpu.make_async_copy(q_hbm.at[:, q_cols(c)], qbuf.at[c], sem_q.at[c]).start()
    send_q(2 * z + 1 - core)

    def send_qs(n, _):
        g = chip(n)
        send_q(2 * g)
        send_q(2 * g + 1)
        return 0

    lax.fori_loop(1, PAIRS, send_qs, 0)

    def line(j, t, bb):
        return kv[j][t].at[pl.ds(lax.rem(bb, SIDE) * SIDE, SIDE)]

    def half(j, bb, which):
        return kv[j][0].at[pl.ds(lax.rem(bb, SIDE) * SIDE, SIDE), which]

    def tile(j, aa):
        return kv[j][0].at[b * SIDE + lax.rem(aa, SIDE)]

    def tile_half(j, aa, which):
        return kv[j][0].at[b * SIDE + lax.rem(aa, SIDE), which]

    def aside(j, bb):
        send(line(j, 0, bb), line(j, 1, bb), ss.at[j], rs.at[j], sib)

    def event1(j):
        wait(own.at[j], sem_own.at[j])
        send(own.at[j], kv[j][0].at[place], s1.at[j, 0], r1.at[j, 0], a_next)
        send(own.at[j], kv[j][0].at[place], s1.at[j, 1], r1.at[j, 1], a_prev)
        pltpu.make_async_copy(own.at[j], kv[j][0].at[place], sem_cp.at[j]).start()

    def event2(j):
        wait(tile(j, a + 3), r1.at[j, 0])
        send(tile_half(j, a + 3, 0), tile_half(j, a + 3, 0), s2.at[j, 0], r2.at[j, 0], a_next)
        wait(tile(j, a + 1), r1.at[j, 1])
        send(tile_half(j, a + 1, 1), tile_half(j, a + 1, 1), s2.at[j, 1], r2.at[j, 1], a_prev)

    def event3(j):
        wait(tile_half(j, a + 2, 0), r2.at[j, 0])
        wait(tile_half(j, a + 2, 1), r2.at[j, 1])
        wait(kv[j][0].at[place], sem_cp.at[j])
        send(line(j, 0, b), line(j, 0, b), s3.at[j, 0], r3.at[j, 0], b_next)
        send(line(j, 0, b), line(j, 0, b), s3.at[j, 1], r3.at[j, 1], b_prev)
        aside(j, b)

    def event4(j):
        wait(line(j, 0, b + 3), r3.at[j, 0])
        send(half(j, b + 3, 0), half(j, b + 3, 0), s4.at[j, 0], r4.at[j, 0], b_next)
        wait(line(j, 0, b + 1), r3.at[j, 1])
        send(half(j, b + 1, 1), half(j, b + 1, 1), s4.at[j, 1], r4.at[j, 1], b_prev)
        aside(j, b + 3)
        aside(j, b + 1)

    def event5(j):
        wait(half(j, b + 2, 0), r4.at[j, 0])
        wait(half(j, b + 2, 1), r4.at[j, 1])
        aside(j, b + 2)

    def events(n):
        for late, event in enumerate((event1, event2, event3, event4, event5)):
            if 0 <= n - late < PAIRS:
                event(n - late)

    parity = (core, 1 - core)

    def tiles_of(j, cc, i):
        parts = []
        for t in range(2):
            span = 2 * j + parity[t]
            limit = jnp.where(span < cc, NB, jnp.where(span == cc, h, 0))
            for n in range(SLOTS):
                e = lst[cc, i, span * SLOTS + n]
                off = jnp.where((e >= 0) & (e < limit), 0.0, OFF)
                e = jnp.clip(e, 0, NB - 1)
                at = jnp.where(parity[t] == 0, e, (e % SIDE) * SIDE + e // SIDE)
                scores = dot(kv[j][t][at, 0], qt[cc, i])
                parts.append((scores, off, kv[j][t][at, 1]))
        return parts

    def absorb(cc, i, parts, first):
        top = jnp.full((1, BLOCK), LOW, F32) if first else m_ref[cc, i]
        m_old = top
        for s, off, _ in parts:
            top = jnp.maximum(top, jnp.max(s, axis=0, keepdims=True) * SCALE - off)
        probs = [jnp.exp2(s * SCALE - (top + off)) for s, off, _ in parts]
        total = jnp.sum(functools.reduce(jnp.add, probs), axis=0, keepdims=True)
        out = None
        for p, (_, _, values) in zip(probs, parts):
            o = dot(values, p.astype(BF16))
            out = o if out is None else out + o
        if not first:
            keep = jnp.exp2(m_old - top)
            total = l_ref[cc, i] * keep + total
            out = acc[cc, i] * keep + out
        return top, total, out

    def later_rows(j, pair):
        for u in range(2):
            for i in range(2):
                cc = 2 * pair + u
                top, total, out = absorb(cc, i, tiles_of(j, cc, i), j == 0)
                m_ref[cc, i] = top
                l_ref[cc, i] = total
                acc[cc, i] = out

    def out_cols(p):
        return pl.ds(pl.multiple_of(p * 2 * HD, 2 * HD), 2 * HD)

    def last_rows(j):
        keys = lax.broadcasted_iota(jnp.int32, (BLOCK, BLOCK), 0)
        toks = lax.broadcasted_iota(jnp.int32, (BLOCK, BLOCK), 1)
        for t in range(2):
            cc = 2 * j + parity[t]
            here = place if t == 0 else mirrored
            for i in range(2):
                scores = jnp.where(keys <= toks, dot(kv[j][t][here, 0], qt[cc, i]), LOW)
                parts = tiles_of(j, cc, i) + [(scores, 0.0, kv[j][t][here, 1])]
                _, total, out = absorb(cc, i, parts, j == 0)
                obuf[cc, :, i * HD:(i + 1) * HD] = (out / total).T.astype(BF16)
        for t in range(2):
            cc = 2 * j + parity[t]

            @pl.when(cc != c)
            def _():
                send(obuf.at[cc], out_ref.at[:, out_cols(c)], sem_o.at[0], sem_o.at[1], (h, cc))

            @pl.when(cc == c)
            def _():
                pltpu.make_async_copy(obuf.at[cc], out_ref.at[:, out_cols(c)], sem_o.at[1]).start()

    def turn(cc):
        wait(qbuf.at[cc], sem_q.at[cc])
        for i in range(2):
            qt[cc, i] = qbuf[cc, :, i * HD:(i + 1) * HD].T

    for n in range(5):
        events(n)
    wait(lst_v, sem_l.at[1])
    pltpu.make_async_copy(lst_v, lst, sem_l.at[3]).start()
    pltpu.make_async_copy(lst_v, lst, sem_l.at[3]).wait()

    plan = {j: {1: 5 + j} for j in range(7)}
    for j in range(PAIRS):
        wait(kv[j][1], rs.at[j])
        marks = plan.get(j, {})
        if j == 0:
            def some(n, _):
                pair = chip(n)
                turn(2 * pair)
                turn(2 * pair + 1)

                @pl.when(pair != 0)
                def _():
                    later_rows(0, pair)

                for at, step in marks.items():
                    @pl.when(n == at)
                    def _():
                        events(step)
                return 0

            lax.fori_loop(0, PAIRS, some, 0)
            last_rows(0)
        else:
            last_rows(j)
            if j + 1 < PAIRS:
                def some(pair, _):
                    later_rows(j, pair)
                    for at, step in marks.items():
                        @pl.when(pair == j + at)
                        def _():
                            events(step)
                    return 0

                lax.fori_loop(j + 1, PAIRS, some, 0)

    wait(out_ref, sem_o.at[1])

    wait(own.at[pl.ds(0, PAIRS - 1), 0], sem_kvs.at[0])
    wait(own.at[pl.ds(0, PAIRS - 1), 1], sem_kvs.at[1])
    wait(lists.at[pl.ds(0, NB - 1)], sem_l.at[0])

    @pl.when(c != h)
    def _():
        wait(lists.at[0], sem_l.at[2])

    wait(qbuf.at[pl.ds(0, SPANS - 1)], sem_qs.at[0])
    wait(obuf.at[pl.ds(0, SPANS - 1)], sem_o.at[0])
    for j in range(PAIRS):
        for n in range(2):
            wait(own.at[j], s1.at[j, n])
            wait(tile_half(j, a, n), s2.at[j, n])
            wait(line(j, 0, b), s3.at[j, n])
            wait(half(j, b, n), s4.at[j, n])
        wait(kv[j][0], ss.at[j])


def body(queries, keys, values, blocks):
    anywhere = pl.BlockSpec(memory_space=pl.ANY)
    vmem = pl.BlockSpec(memory_space=pltpu.VMEM)
    dma = pltpu.SemaphoreType.DMA
    events = [dma((PAIRS, 2)) for _ in range(4)] + [dma((PAIRS,))]
    out = pl.pallas_call(
        kernel,
        out_shape=jax.ShapeDtypeStruct((BLOCK, queries.shape[2]), BF16),
        in_specs=[anywhere, anywhere, vmem, vmem],
        out_specs=vmem,
        scratch_shapes=[pltpu.VMEM((NB, 2, BLOCK, HD), BF16) for _ in range(2 * PAIRS)] + [
            pltpu.VMEM((PAIRS, HD, BLOCK), BF16),
            pltpu.VMEM((PAIRS, 2, BLOCK, HD), BF16),
            pltpu.VMEM((SPANS, BLOCK, 2 * HD), BF16),
            pltpu.VMEM((SPANS, 2, HD, BLOCK), BF16),
            pltpu.VMEM((SPANS, BLOCK, 2 * HD), BF16),
            pltpu.VMEM((SPANS, 2, HD, BLOCK), F32),
            pltpu.VMEM((SPANS, 2, 1, BLOCK), F32),
            pltpu.VMEM((SPANS, 2, 1, BLOCK), F32),
            pltpu.VMEM((NB, 8, 128), jnp.int32),
            pltpu.VMEM((SPANS, 8, 128), jnp.int32),
            pltpu.SMEM((SPANS, 8, 128), jnp.int32),
            dma((PAIRS,)),
            dma((2,)),
            dma((SPANS,)),
            dma((1,)),
            dma((2,)),
            dma((4,)),
            dma((PAIRS,)),
        ] + events + events,
        compiler_params=pltpu.CompilerParams(
            collective_id=0, has_side_effects=True, vmem_limit_bytes=60 * 2**20),
        name="attend",
    )(queries[0], keys[0], values[0], blocks[:, 0])
    return out[None]


def solution(mesh):
    placed = (
        P("blk", "head", None),
        P("blk", "head", None),
        P("blk", "head", None),
        P("head", "blk", None, None),
    )
    return jax.shard_map(
        body, mesh=mesh, in_specs=placed, out_specs=P("blk", "head", None), check_vma=False
    )
```

```python
import functools
import math

import jax
import jax.numpy as jnp
from jax import lax
from jax.experimental import pallas as pl
from jax.experimental.pallas import tpu as pltpu
from jax.sharding import PartitionSpec as P

HD = 128
BLOCK = 128
SLOTS = 3
NB = 16
SPANS = 16
PAIRS = 8
SIDE = 4
F32 = jnp.float32
BF16 = jnp.bfloat16
LAGS = (-1, 0, 1, 3, 4)
LOW = -1e30
OFF = 2e30
SCALE = HD ** (-0.5) * math.log2(math.e)
MESH = pl.DeviceIdType.MESH


def dot(a, b):
    return jnp.dot(a, b, preferred_element_type=F32)


def kernel(q_hbm, k_hbm, v_hbm, b_hbm, out_ref, *scratch):
    kv = [[scratch[j * 2 + t] for t in range(2)] for j in range(PAIRS)]
    (v_ref, b_ref, vt, own, qbuf, qt, obuf, acc, m_ref, l_ref, lists, lst_v, lst,
     sem_own, sem_kvs, sem_q, sem_qs, sem_o, sem_l, sem_cp,
     sem_in, r1, r2, r3, r4, rs, s1, s2, s3, s4, ss) = scratch[2 * PAIRS:]
    h = lax.axis_index("head")
    c = lax.axis_index("blk")
    z, core = c // 2, c % 2
    x, y = h % SIDE, h // SIDE
    sib = (h, 2 * z + 1 - core)
    a = jnp.where(core == 0, x, y)
    b = jnp.where(core == 0, y, x)
    place = b * SIDE + a
    mirrored = a * SIDE + b

    def device(aa, bb):
        aa, bb = lax.rem(aa, SIDE), lax.rem(bb, SIDE)
        return (jnp.where(core == 0, bb * SIDE + aa, aa * SIDE + bb), c)

    a_next, a_prev = device(a + 1, b), device(a + SIDE - 1, b)
    b_next, b_prev = device(a, b + 1), device(a, b + SIDE - 1)

    def wait(ref, sem):
        pltpu.make_async_copy(ref, ref, sem).wait()

    def send(src, dst, s_sem, r_sem, dev):
        pltpu.make_async_remote_copy(
            src_ref=src, dst_ref=dst, send_sem=s_sem, recv_sem=r_sem,
            device_id=dev, device_id_type=MESH).start()

    fetch_v = pltpu.make_async_copy(v_hbm, v_ref, sem_in.at[0])
    fetch_b = pltpu.make_async_copy(b_hbm, b_ref, sem_in.at[1])
    fetch_v.start()
    fetch_b.start()

    barrier = pltpu.get_barrier_semaphore()

    def hello(dev):
        pl.semaphore_signal(barrier, inc=1, device_id=dev, device_id_type=MESH)

    def greet(j, _):
        other = lax.rem(c + j, SPANS)
        hello((h, other))
        hello((c, other))
        return 0

    lax.fori_loop(1, SPANS, greet, 0)
    for dev in (a_next, a_prev, b_next, b_prev):
        hello(dev)

    @pl.when(c != h)
    def _():
        hello((c, c))

    lists[...] = jnp.zeros(lists.shape, jnp.int32)
    fetch_v.wait()
    fetch_b.wait()
    pl.semaphore_wait(barrier, 34 + jnp.where(c != h, 1, 0))

    def chip(n):
        away = jnp.where(n % 2 == 1, (n + 1) // 2, PAIRS - n // 2)
        return lax.rem(z + away, PAIRS)

    def key_cols(g):
        return pl.ds(pl.multiple_of(g * HD, HD), HD)

    def send_k(n, _):
        g = chip(n)
        send(k_hbm.at[:, key_cols(g)], own.at[z, 0], sem_kvs.at[0], sem_own.at[z], (h, 2 * g + core))
        return 0

    def send_v(n, _):
        g = chip(n)
        vt[g] = v_ref[:, key_cols(g)].T
        send(vt.at[g], own.at[z, 1], sem_kvs.at[1], sem_own.at[z], (h, 2 * g + core))
        return 0

    lax.fori_loop(1, PAIRS, send_k, 0)
    pltpu.make_async_copy(k_hbm.at[:, key_cols(z)], own.at[z, 0], sem_own.at[z]).start()
    lax.fori_loop(1, PAIRS, send_v, 0)
    vt[z] = v_ref[:, key_cols(z)].T
    pltpu.make_async_copy(vt.at[z], own.at[z, 1], sem_own.at[z]).start()

    for n in range(NB):
        lists[n, 0:2, 0:SPANS * SLOTS] = b_ref[:, n, :]

    def send_list(j, _):
        p = lax.rem(h + j, NB)
        send(lists.at[p], lst_v.at[c], sem_l.at[0], sem_l.at[1], (p, h))
        return 0

    lax.fori_loop(1, NB, send_list, 0)

    @pl.when(c != h)
    def _():
        send(lists.at[h], lst_v.at[c], sem_l.at[2], sem_l.at[1], (h, h))

    @pl.when(c == h)
    def _():
        pltpu.make_async_copy(lists.at[h], lst_v.at[c], sem_l.at[1]).start()

    def q_cols(p):
        return pl.ds(pl.multiple_of(p * 2 * HD, 2 * HD), 2 * HD)

    def send_q(p):
        send(q_hbm.at[:, q_cols(p)], qbuf.at[c], sem_qs.at[0], sem_q.at[c], (h, p))

    pltpu.make_async_copy(q_hbm.at[:, q_cols(c)], qbuf.at[c], sem_q.at[c]).start()
    send_q(2 * z + 1 - core)

    def send_qs(n, _):
        g = chip(n)
        send_q(2 * g)
        send_q(2 * g + 1)
        return 0

    lax.fori_loop(1, PAIRS, send_qs, 0)

    def line(j, t, bb):
        return kv[j][t].at[pl.ds(lax.rem(bb, SIDE) * SIDE, SIDE)]

    def half(j, bb, which):
        return kv[j][0].at[pl.ds(lax.rem(bb, SIDE) * SIDE, SIDE), which]

    def tile(j, aa):
        return kv[j][0].at[b * SIDE + lax.rem(aa, SIDE)]

    def tile_half(j, aa, which):
        return kv[j][0].at[b * SIDE + lax.rem(aa, SIDE), which]

    def aside(j, bb):
        send(line(j, 0, bb), line(j, 1, bb), ss.at[j], rs.at[j], sib)

    def event1(j):
        wait(own.at[j], sem_own.at[j])
        send(own.at[j], kv[j][0].at[place], s1.at[j, 0], r1.at[j, 0], a_next)
        send(own.at[j], kv[j][0].at[place], s1.at[j, 1], r1.at[j, 1], a_prev)
        pltpu.make_async_copy(own.at[j], kv[j][0].at[place], sem_cp.at[j]).start()

    def event2(j):
        wait(tile(j, a + 3), r1.at[j, 0])
        send(tile_half(j, a + 3, 0), tile_half(j, a + 3, 0), s2.at[j, 0], r2.at[j, 0], a_next)
        wait(tile(j, a + 1), r1.at[j, 1])
        send(tile_half(j, a + 1, 1), tile_half(j, a + 1, 1), s2.at[j, 1], r2.at[j, 1], a_prev)

    def event3(j):
        wait(tile_half(j, a + 2, 0), r2.at[j, 0])
        wait(tile_half(j, a + 2, 1), r2.at[j, 1])
        wait(kv[j][0].at[place], sem_cp.at[j])
        send(line(j, 0, b), line(j, 0, b), s3.at[j, 0], r3.at[j, 0], b_next)
        send(line(j, 0, b), line(j, 0, b), s3.at[j, 1], r3.at[j, 1], b_prev)
        aside(j, b)

    def event4(j):
        wait(line(j, 0, b + 3), r3.at[j, 0])
        send(half(j, b + 3, 0), half(j, b + 3, 0), s4.at[j, 0], r4.at[j, 0], b_next)
        wait(line(j, 0, b + 1), r3.at[j, 1])
        send(half(j, b + 1, 1), half(j, b + 1, 1), s4.at[j, 1], r4.at[j, 1], b_prev)
        aside(j, b + 3)
        aside(j, b + 1)

    def event5(j):
        wait(half(j, b + 2, 0), r4.at[j, 0])
        wait(half(j, b + 2, 1), r4.at[j, 1])
        aside(j, b + 2)

    def advance(n, kinds=(1, 2, 3, 4, 5)):
        steps = zip(LAGS, (event1, event2, event3, event4, event5))
        for kind, (late, event) in enumerate(steps, 1):
            if kind in kinds and 0 <= n - late < PAIRS:
                event(n - late)

    parity = (core, 1 - core)

    def tiles_of(j, cc, i):
        parts = []
        for t in range(2):
            span = 2 * j + parity[t]
            limit = jnp.where(span < cc, NB, jnp.where(span == cc, h, 0))
            for n in range(SLOTS):
                e = lst[cc, i, span * SLOTS + n]
                off = jnp.where((e >= 0) & (e < limit), 0.0, OFF)
                e = jnp.clip(e, 0, NB - 1)
                at = jnp.where(parity[t] == 0, e, (e % SIDE) * SIDE + e // SIDE)
                scores = dot(kv[j][t][at, 0], qt[cc, i])
                parts.append((scores, off, kv[j][t][at, 1]))
        return parts

    def absorb(cc, i, parts, first):
        top = jnp.full((1, BLOCK), LOW, F32) if first else m_ref[cc, i]
        m_old = top
        for s, off, _ in parts:
            top = jnp.maximum(top, jnp.max(s, axis=0, keepdims=True) * SCALE - off)
        probs = [jnp.exp2(s * SCALE - (top + off)) for s, off, _ in parts]
        total = jnp.sum(functools.reduce(jnp.add, probs), axis=0, keepdims=True)
        out = None
        for p, (_, _, values) in zip(probs, parts):
            o = dot(values, p.astype(BF16))
            out = o if out is None else out + o
        if not first:
            keep = jnp.exp2(m_old - top)
            total = l_ref[cc, i] * keep + total
            out = acc[cc, i] * keep + out
        return top, total, out

    def later_rows(j, pair):
        for u in range(2):
            for i in range(2):
                cc = 2 * pair + u
                top, total, out = absorb(cc, i, tiles_of(j, cc, i), j == 0)
                m_ref[cc, i] = top
                l_ref[cc, i] = total
                acc[cc, i] = out

    def out_cols(p):
        return pl.ds(pl.multiple_of(p * 2 * HD, 2 * HD), 2 * HD)

    def last_rows(j):
        keys = lax.broadcasted_iota(jnp.int32, (BLOCK, BLOCK), 0)
        toks = lax.broadcasted_iota(jnp.int32, (BLOCK, BLOCK), 1)
        for t in range(2):
            cc = 2 * j + parity[t]
            here = place if t == 0 else mirrored
            for i in range(2):
                scores = jnp.where(keys <= toks, dot(kv[j][t][here, 0], qt[cc, i]), LOW)
                parts = tiles_of(j, cc, i) + [(scores, 0.0, kv[j][t][here, 1])]
                _, total, out = absorb(cc, i, parts, j == 0)
                obuf[cc, :, i * HD:(i + 1) * HD] = (out / total).T.astype(BF16)
        for t in range(2):
            cc = 2 * j + parity[t]

            @pl.when(cc != c)
            def _():
                send(obuf.at[cc], out_ref.at[:, out_cols(c)], sem_o.at[0], sem_o.at[1], (h, cc))

            @pl.when(cc == c)
            def _():
                pltpu.make_async_copy(obuf.at[cc], out_ref.at[:, out_cols(c)], sem_o.at[1]).start()

    def turn(cc):
        wait(qbuf.at[cc], sem_q.at[cc])
        for i in range(2):
            qt[cc, i] = qbuf[cc, :, i * HD:(i + 1) * HD].T

    for n in range(-1, 5):
        advance(n)
    wait(lst_v, sem_l.at[1])
    pltpu.make_async_copy(lst_v, lst, sem_l.at[3]).start()
    pltpu.make_async_copy(lst_v, lst, sem_l.at[3]).wait()

    for j in range(PAIRS):
        wait(kv[j][1], rs.at[j])
        advance(j + 5, (1, 2, 3, 4))
        if j == 0:
            def some(n, _):
                pair = chip(n)
                turn(2 * pair)
                turn(2 * pair + 1)

                @pl.when(pair != 0)
                def _():
                    later_rows(0, pair)

                @pl.when(n == 2)
                def _():
                    advance(j + 5, (5,))
                return 0

            lax.fori_loop(0, PAIRS, some, 0)
            last_rows(0)
        else:
            last_rows(j)
            advance(j + 5, (5,))

            def some(pair, _):
                later_rows(j, pair)
                return 0

            lax.fori_loop(j + 1, PAIRS, some, 0)

    wait(out_ref, sem_o.at[1])

    wait(own.at[pl.ds(0, PAIRS - 1), 0], sem_kvs.at[0])
    wait(own.at[pl.ds(0, PAIRS - 1), 1], sem_kvs.at[1])
    wait(lists.at[pl.ds(0, NB - 1)], sem_l.at[0])

    @pl.when(c != h)
    def _():
        wait(lists.at[0], sem_l.at[2])

    wait(qbuf.at[pl.ds(0, SPANS - 1)], sem_qs.at[0])
    wait(obuf.at[pl.ds(0, SPANS - 1)], sem_o.at[0])
    for j in range(PAIRS):
        for n in range(2):
            wait(own.at[j], s1.at[j, n])
            wait(tile_half(j, a, n), s2.at[j, n])
            wait(line(j, 0, b), s3.at[j, n])
            wait(half(j, b, n), s4.at[j, n])
        wait(kv[j][0], ss.at[j])


def body(queries, keys, values, blocks):
    hbm = pl.BlockSpec(memory_space=pltpu.HBM)
    vmem = pl.BlockSpec(memory_space=pltpu.VMEM)
    dma = pltpu.SemaphoreType.DMA
    events = [dma((PAIRS, 2)) for _ in range(4)] + [dma((PAIRS,))]
    out = pl.pallas_call(
        kernel,
        out_shape=jax.ShapeDtypeStruct((BLOCK, queries.shape[2]), BF16),
        in_specs=[hbm] * 4,
        out_specs=hbm,
        scratch_shapes=[pltpu.VMEM((NB, 2, BLOCK, HD), BF16) for _ in range(2 * PAIRS)] + [
            pltpu.VMEM((BLOCK, PAIRS * HD), BF16),
            pltpu.VMEM((2, NB, SPANS * SLOTS), jnp.int32),
            pltpu.VMEM((PAIRS, HD, BLOCK), BF16),
            pltpu.VMEM((PAIRS, 2, BLOCK, HD), BF16),
            pltpu.VMEM((SPANS, BLOCK, 2 * HD), BF16),
            pltpu.VMEM((SPANS, 2, HD, BLOCK), BF16),
            pltpu.VMEM((SPANS, BLOCK, 2 * HD), BF16),
            pltpu.VMEM((SPANS, 2, HD, BLOCK), F32),
            pltpu.VMEM((SPANS, 2, 1, BLOCK), F32),
            pltpu.VMEM((SPANS, 2, 1, BLOCK), F32),
            pltpu.VMEM((NB, 8, 128), jnp.int32),
            pltpu.VMEM((SPANS, 8, 128), jnp.int32),
            pltpu.SMEM((SPANS, 8, 128), jnp.int32),
            dma((PAIRS,)),
            dma((2,)),
            dma((SPANS,)),
            dma((1,)),
            dma((2,)),
            dma((4,)),
            dma((PAIRS,)),
            dma((2,)),
        ] + events + events,
        compiler_params=pltpu.CompilerParams(
            collective_id=0, has_side_effects=True, vmem_limit_bytes=60 * 2**20),
        name="attend",
    )(queries[0], keys[0], values[0], blocks[:, 0])
    return out[None]


def solution(mesh):
    placed = (
        P("blk", "head", None),
        P("blk", "head", None),
        P("blk", "head", None),
        P("head", "blk", None, None),
    )
    return jax.shard_map(
        body, mesh=mesh, in_specs=placed, out_specs=P("blk", "head", None), check_vma=False
    )
```

```python
import functools
import math

import jax
import jax.numpy as jnp
from jax import lax
from jax.experimental import pallas as pl
from jax.experimental.pallas import tpu as pltpu
from jax.sharding import PartitionSpec as P

HD = 128
BLOCK = 128
SLOTS = 3
NB = 16
SPANS = 16
PAIRS = 8
SIDE = 4
F32 = jnp.float32
BF16 = jnp.bfloat16
LAGS = (-1, 0, 1, 3, 4)
LOW = -1e30
OFF = 2e30
SCALE = HD ** (-0.5) * math.log2(math.e)
MESH = pl.DeviceIdType.MESH


def dot(a, b):
    return jnp.dot(a, b, preferred_element_type=F32)


def kernel(q_hbm, k_hbm, v_hbm, b_hbm, out_ref, *scratch):
    kv = [[scratch[j * 2 + t] for t in range(2)] for j in range(PAIRS)]
    (v_ref, b_ref, vt, own, qbuf, qt, obuf, acc, m_ref, l_ref, lists, lst_v, lst,
     sem_own, sem_kvs, sem_q, sem_qs, sem_o, sem_l, sem_cp,
     sem_in, r1, r2, r3, r4, rs, s1, s2, s3, s4, ss) = scratch[2 * PAIRS:]
    h = lax.axis_index("head")
    c = lax.axis_index("blk")
    z, core = c // 2, c % 2
    x, y = h % SIDE, h // SIDE
    sib = (h, 2 * z + 1 - core)
    a = jnp.where(core == 0, x, y)
    b = jnp.where(core == 0, y, x)
    place = b * SIDE + a
    mirrored = a * SIDE + b

    def device(aa, bb):
        aa, bb = lax.rem(aa, SIDE), lax.rem(bb, SIDE)
        return (jnp.where(core == 0, bb * SIDE + aa, aa * SIDE + bb), c)

    a_next, a_prev = device(a + 1, b), device(a + SIDE - 1, b)
    b_next, b_prev = device(a, b + 1), device(a, b + SIDE - 1)

    def wait(ref, sem):
        pltpu.make_async_copy(ref, ref, sem).wait()

    def send(src, dst, s_sem, r_sem, dev):
        pltpu.make_async_remote_copy(
            src_ref=src, dst_ref=dst, send_sem=s_sem, recv_sem=r_sem,
            device_id=dev, device_id_type=MESH).start()

    fetch_v = pltpu.make_async_copy(v_hbm, v_ref, sem_in.at[0])
    fetch_b = pltpu.make_async_copy(b_hbm, b_ref, sem_in.at[1])
    fetch_v.start()
    fetch_b.start()

    barrier = pltpu.get_barrier_semaphore()

    def hello(dev):
        pl.semaphore_signal(barrier, inc=1, device_id=dev, device_id_type=MESH)

    def greet(j, _):
        other = lax.rem(c + j, SPANS)
        hello((h, other))
        hello((c, other))
        return 0

    lax.fori_loop(1, SPANS, greet, 0)
    for dev in (a_next, a_prev, b_next, b_prev):
        hello(dev)

    @pl.when(c != h)
    def _():
        hello((c, c))

    lists[...] = jnp.zeros(lists.shape, jnp.int32)
    fetch_v.wait()
    fetch_b.wait()
    pl.semaphore_wait(barrier, 34 + jnp.where(c != h, 1, 0))

    def chip(n):
        away = jnp.where(n % 2 == 1, (n + 1) // 2, PAIRS - n // 2)
        return lax.rem(z + away, PAIRS)

    def key_cols(g):
        return pl.ds(pl.multiple_of(g * HD, HD), HD)

    def send_k(n, _):
        g = chip(n)
        send(k_hbm.at[:, key_cols(g)], own.at[z, 0], sem_kvs.at[0], sem_own.at[z], (h, 2 * g + core))
        return 0

    def send_v(n, _):
        g = chip(n)
        vt[g] = v_ref[:, key_cols(g)].T
        send(vt.at[g], own.at[z, 1], sem_kvs.at[1], sem_own.at[z], (h, 2 * g + core))
        return 0

    lax.fori_loop(1, PAIRS, send_k, 0)
    pltpu.make_async_copy(k_hbm.at[:, key_cols(z)], own.at[z, 0], sem_own.at[z]).start()
    lax.fori_loop(1, PAIRS, send_v, 0)
    vt[z] = v_ref[:, key_cols(z)].T
    pltpu.make_async_copy(vt.at[z], own.at[z, 1], sem_own.at[z]).start()

    for n in range(NB):
        lists[n, 0:2, 0:SPANS * SLOTS] = b_ref[:, n, :]

    def send_list(j, _):
        p = lax.rem(h + j, NB)
        send(lists.at[p], lst_v.at[c], sem_l.at[0], sem_l.at[1], (p, h))
        return 0

    lax.fori_loop(1, NB, send_list, 0)

    @pl.when(c != h)
    def _():
        send(lists.at[h], lst_v.at[c], sem_l.at[2], sem_l.at[1], (h, h))

    @pl.when(c == h)
    def _():
        pltpu.make_async_copy(lists.at[h], lst_v.at[c], sem_l.at[1]).start()

    def q_cols(p):
        return pl.ds(pl.multiple_of(p * 2 * HD, 2 * HD), 2 * HD)

    def send_q(p):
        send(q_hbm.at[:, q_cols(p)], qbuf.at[c], sem_qs.at[0], sem_q.at[c], (h, p))

    pltpu.make_async_copy(q_hbm.at[:, q_cols(c)], qbuf.at[c], sem_q.at[c]).start()
    send_q(2 * z + 1 - core)

    def send_qs(n, _):
        g = chip(n)
        send_q(2 * g)
        send_q(2 * g + 1)
        return 0

    lax.fori_loop(1, PAIRS, send_qs, 0)

    def line(j, t, bb):
        return kv[j][t].at[pl.ds(lax.rem(bb, SIDE) * SIDE, SIDE)]

    def half(j, bb, which):
        return kv[j][0].at[pl.ds(lax.rem(bb, SIDE) * SIDE, SIDE), which]

    def tile(j, aa):
        return kv[j][0].at[b * SIDE + lax.rem(aa, SIDE)]

    def tile_half(j, aa, which):
        return kv[j][0].at[b * SIDE + lax.rem(aa, SIDE), which]

    def aside(j, bb):
        send(line(j, 0, bb), line(j, 1, bb), ss.at[j], rs.at[j], sib)

    def event1(j):
        wait(own.at[j], sem_own.at[j])
        send(own.at[j], kv[j][0].at[place], s1.at[j, 0], r1.at[j, 0], a_next)
        send(own.at[j], kv[j][0].at[place], s1.at[j, 1], r1.at[j, 1], a_prev)
        pltpu.make_async_copy(own.at[j], kv[j][0].at[place], sem_cp.at[j]).start()

    def event2(j):
        wait(tile(j, a + 3), r1.at[j, 0])
        send(tile_half(j, a + 3, 0), tile_half(j, a + 3, 0), s2.at[j, 0], r2.at[j, 0], a_next)
        wait(tile(j, a + 1), r1.at[j, 1])
        send(tile_half(j, a + 1, 1), tile_half(j, a + 1, 1), s2.at[j, 1], r2.at[j, 1], a_prev)

    def event3(j):
        wait(tile_half(j, a + 2, 0), r2.at[j, 0])
        wait(tile_half(j, a + 2, 1), r2.at[j, 1])
        wait(kv[j][0].at[place], sem_cp.at[j])
        send(line(j, 0, b), line(j, 0, b), s3.at[j, 0], r3.at[j, 0], b_next)
        send(line(j, 0, b), line(j, 0, b), s3.at[j, 1], r3.at[j, 1], b_prev)
        aside(j, b)

    def event4(j):
        wait(line(j, 0, b + 3), r3.at[j, 0])
        send(half(j, b + 3, 0), half(j, b + 3, 0), s4.at[j, 0], r4.at[j, 0], b_next)
        wait(line(j, 0, b + 1), r3.at[j, 1])
        send(half(j, b + 1, 1), half(j, b + 1, 1), s4.at[j, 1], r4.at[j, 1], b_prev)
        aside(j, b + 3)
        aside(j, b + 1)

    def event5(j):
        wait(half(j, b + 2, 0), r4.at[j, 0])
        wait(half(j, b + 2, 1), r4.at[j, 1])
        aside(j, b + 2)

    def advance(n, kinds=(1, 2, 3, 4, 5)):
        steps = zip(LAGS, (event1, event2, event3, event4, event5))
        for kind, (late, event) in enumerate(steps, 1):
            if kind in kinds and 0 <= n - late < PAIRS:
                event(n - late)

    parity = (core, 1 - core)

    def tiles_of(j, cc, i):
        parts = []
        for t in range(2):
            span = 2 * j + parity[t]
            limit = jnp.where(span < cc, NB, jnp.where(span == cc, h, 0))
            for n in range(SLOTS):
                e = lst[cc, i, span * SLOTS + n]
                off = jnp.where((e >= 0) & (e < limit), 0.0, OFF)
                e = jnp.clip(e, 0, NB - 1)
                at = jnp.where(parity[t] == 0, e, (e % SIDE) * SIDE + e // SIDE)
                scores = dot(kv[j][t][at, 0], qt[cc, i])
                parts.append((scores, off, kv[j][t][at, 1]))
        return parts

    def absorb(cc, i, parts, first):
        top = jnp.full((1, BLOCK), LOW, F32) if first else m_ref[cc, i]
        m_old = top
        for s, off, _ in parts:
            top = jnp.maximum(top, jnp.max(s, axis=0, keepdims=True) * SCALE - off)
        probs = [jnp.exp2(s * SCALE - (top + off)) for s, off, _ in parts]
        total = jnp.sum(functools.reduce(jnp.add, probs), axis=0, keepdims=True)
        out = None
        for p, (_, _, values) in zip(probs, parts):
            o = dot(values, p.astype(BF16))
            out = o if out is None else out + o
        if not first:
            keep = jnp.exp2(m_old - top)
            total = l_ref[cc, i] * keep + total
            out = acc[cc, i] * keep + out
        return top, total, out

    def later_rows(j, pair):
        for u in range(2):
            for i in range(2):
                cc = 2 * pair + u
                top, total, out = absorb(cc, i, tiles_of(j, cc, i), j == 0)
                m_ref[cc, i] = top
                l_ref[cc, i] = total
                acc[cc, i] = out

    def out_cols(p):
        return pl.ds(pl.multiple_of(p * 2 * HD, 2 * HD), 2 * HD)

    def last_rows(j):
        keys = lax.broadcasted_iota(jnp.int32, (BLOCK, BLOCK), 0)
        toks = lax.broadcasted_iota(jnp.int32, (BLOCK, BLOCK), 1)
        for t in range(2):
            cc = 2 * j + parity[t]
            here = place if t == 0 else mirrored
            for i in range(2):
                scores = jnp.where(keys <= toks, dot(kv[j][t][here, 0], qt[cc, i]), LOW)
                parts = tiles_of(j, cc, i) + [(scores, 0.0, kv[j][t][here, 1])]
                _, total, out = absorb(cc, i, parts, j == 0)
                obuf[cc, :, i * HD:(i + 1) * HD] = (out / total).T.astype(BF16)

            @pl.when(cc != c)
            def _():
                send(obuf.at[cc], out_ref.at[:, out_cols(c)], sem_o.at[0], sem_o.at[1], (h, cc))

            @pl.when(cc == c)
            def _():
                pltpu.make_async_copy(obuf.at[cc], out_ref.at[:, out_cols(c)], sem_o.at[1]).start()

    def turn(cc):
        wait(qbuf.at[cc], sem_q.at[cc])
        for i in range(2):
            qt[cc, i] = qbuf[cc, :, i * HD:(i + 1) * HD].T

    for n in range(-1, 5):
        advance(n)
    wait(lst_v, sem_l.at[1])
    pltpu.make_async_copy(lst_v, lst, sem_l.at[3]).start()
    pltpu.make_async_copy(lst_v, lst, sem_l.at[3]).wait()

    for j in range(PAIRS):
        wait(kv[j][1], rs.at[j])
        advance(j + 5, (1, 2, 3, 4))
        if j == 0:
            def some(n, _):
                pair = chip(n)
                turn(2 * pair)
                turn(2 * pair + 1)

                @pl.when(pair != 0)
                def _():
                    later_rows(0, pair)

                @pl.when(n == 2)
                def _():
                    advance(j + 5, (5,))
                return 0

            lax.fori_loop(0, PAIRS, some, 0)
            last_rows(0)
        else:
            last_rows(j)
            advance(j + 5, (5,))

            def some(pair, _):
                later_rows(j, pair)
                return 0

            lax.fori_loop(j + 1, PAIRS, some, 0)

    wait(out_ref, sem_o.at[1])

    wait(own.at[pl.ds(0, PAIRS - 1), 0], sem_kvs.at[0])
    wait(own.at[pl.ds(0, PAIRS - 1), 1], sem_kvs.at[1])
    wait(lists.at[pl.ds(0, NB - 1)], sem_l.at[0])

    @pl.when(c != h)
    def _():
        wait(lists.at[0], sem_l.at[2])

    wait(qbuf.at[pl.ds(0, SPANS - 1)], sem_qs.at[0])
    wait(obuf.at[pl.ds(0, SPANS - 1)], sem_o.at[0])
    for j in range(PAIRS):
        for n in range(2):
            wait(own.at[j], s1.at[j, n])
            wait(tile_half(j, a, n), s2.at[j, n])
            wait(line(j, 0, b), s3.at[j, n])
            wait(half(j, b, n), s4.at[j, n])
        wait(kv[j][0], ss.at[j])


def body(queries, keys, values, blocks):
    hbm = pl.BlockSpec(memory_space=pltpu.HBM)
    vmem = pl.BlockSpec(memory_space=pltpu.VMEM)
    dma = pltpu.SemaphoreType.DMA
    events = [dma((PAIRS, 2)) for _ in range(4)] + [dma((PAIRS,))]
    out = pl.pallas_call(
        kernel,
        out_shape=jax.ShapeDtypeStruct((BLOCK, queries.shape[2]), BF16),
        in_specs=[hbm] * 4,
        out_specs=hbm,
        scratch_shapes=[pltpu.VMEM((NB, 2, BLOCK, HD), BF16) for _ in range(2 * PAIRS)] + [
            pltpu.VMEM((BLOCK, PAIRS * HD), BF16),
            pltpu.VMEM((2, NB, SPANS * SLOTS), jnp.int32),
            pltpu.VMEM((PAIRS, HD, BLOCK), BF16),
            pltpu.VMEM((PAIRS, 2, BLOCK, HD), BF16),
            pltpu.VMEM((SPANS, BLOCK, 2 * HD), BF16),
            pltpu.VMEM((SPANS, 2, HD, BLOCK), BF16),
            pltpu.VMEM((SPANS, BLOCK, 2 * HD), BF16),
            pltpu.VMEM((SPANS, 2, HD, BLOCK), F32),
            pltpu.VMEM((SPANS, 2, 1, BLOCK), F32),
            pltpu.VMEM((SPANS, 2, 1, BLOCK), F32),
            pltpu.VMEM((NB, 8, 128), jnp.int32),
            pltpu.VMEM((SPANS, 8, 128), jnp.int32),
            pltpu.SMEM((SPANS, 8, 128), jnp.int32),
            dma((PAIRS,)),
            dma((2,)),
            dma((SPANS,)),
            dma((1,)),
            dma((2,)),
            dma((4,)),
            dma((PAIRS,)),
            dma((2,)),
        ] + events + events,
        compiler_params=pltpu.CompilerParams(
            collective_id=0, has_side_effects=True, vmem_limit_bytes=60 * 2**20),
        name="attend",
    )(queries[0], keys[0], values[0], blocks[:, 0])
    return out[None]


def solution(mesh):
    placed = (
        P("blk", "head", None),
        P("blk", "head", None),
        P("blk", "head", None),
        P("head", "blk", None, None),
    )
    return jax.shard_map(
        body, mesh=mesh, in_specs=placed, out_specs=P("blk", "head", None), check_vma=False
    )
```
